128 devices in a mesh: hst: 8 (over y, core), chip: 16 (over z, x).
Axes of the slice: x: 4, y: 4, z: 4, core: 2. Of those that a mesh axis runs over, the one named last changes fastest.
Arguments:
- inputs: bfloat16 [128, 4096], P(('hst', 'chip')), may hold values from -6 to 6
- values: bfloat16 [131072, 4096], P(('hst', 'chip')), may hold values from -6 to 6
- slots: int32 [128, 4, 32], P(('hst', 'chip')), may hold values from 0 to 131071, as said below
- weights: bfloat16 [128, 4, 32], P(('hst', 'chip')), may hold values from -0.59765625 to 0.59765625
Outputs:
- mixed: bfloat16 [128, 4096], P(('hst', 'chip'))
The draws below stay inside these ranges and needn't reach their ends.
Inputs may be any that keep to these rules, and one draw needn't show every extreme that they name: `slots`: of the 128 picks of the rows on one device, at most 4 name value rows held by one device; some devices' value rows are named that often by every device.
All inputs are finite; a program needn't handle non-finite values.
Results may differ from the reference program's by a relative error of at most 0.009.
Values may be sent and summed in bfloat16 or wider, within the bound.
No kernel may reach another device: no remote copies, remote signals or barrier semaphores. Data moves between devices by JAX's collectives and lax.ppermute only.
A program may use at most 64 MiB of HBM per device.

```python
import jax
import jax.numpy as jnp
from jax import lax

D = 4096
H = 4
K = 32
SLOT_DEV = 1024
OWNERS = 128
QUERIES = 128
SLOTS = 131072
PICKS = 128
CAP = 4
HOT = 8


def draw_slots(key, part):
    key = jax.random.fold_in(key, 7)
    middle = (jax.random.permutation(jax.random.fold_in(key, 1), OWNERS - 2) + 1).astype(jnp.int32)
    ordering = jnp.concatenate([middle[:HOT], jnp.array([OWNERS - 1, 0], jnp.int32), middle[HOT:]])
    index = jnp.arange(PICKS, dtype=jnp.int32)
    placing = jnp.where(index < HOT * CAP, index // CAP, HOT + (index - HOT * CAP) % (OWNERS - HOT))
    owner_id = ordering[placing]
    local_row = jax.random.randint(jax.random.fold_in(key, 2), (OWNERS, PICKS), 0, SLOT_DEV).astype(jnp.int32)
    local_row = local_row.at[:, HOT * CAP].set(SLOT_DEV - 1).at[:, HOT * CAP + 1].set(0)
    chosen = owner_id[None, :] * SLOT_DEV + local_row
    shuffles = jax.vmap(lambda inner: jax.random.permutation(inner, PICKS))(jax.random.split(jax.random.fold_in(key, 3), OWNERS))
    mixed_order = jnp.take_along_axis(chosen, shuffles.astype(jnp.int32), axis=1)
    return mixed_order.reshape(QUERIES, H, K).astype(jnp.int32)


def block_scale(rng, dims, pieces, least, largest):
    gain = 1.0
    for axis_at, shards_of in pieces:
        steps = jax.random.uniform(jax.random.fold_in(jax.random.fold_in(rng, 6), axis_at), (shards_of,), jnp.float32, least / len(pieces), largest / len(pieces))
        gain = gain * jnp.repeat(jnp.exp(steps), dims[axis_at] // shards_of).reshape((-1,) + (1,) * (len(dims) - 1 - axis_at))
    return gain


def centred(key, shape, spread, bound, shards=(), held_as=jnp.bfloat16):
    loudness = block_scale(key, shape, shards, -0.22, 0.18) if shards else 1.0
    values = jax.random.normal(key, shape, jnp.float32) * spread * loudness
    return jnp.minimum(jnp.maximum(values, -bound), bound).astype(held_as)


def setup_inputs(seed: int = 0) -> dict:
    streams_of = jax.random.split(jax.random.key(seed), 5)
    return {
        "inputs": centred(streams_of[0], (QUERIES, D), 1.0, 6.0, ((0, 128),)),
        "values": centred(streams_of[1], (SLOTS, D), 1.0, 6.0, ((0, 128),)),
        "slots": draw_slots(jax.random.fold_in(streams_of[4], 71), 0),
        "weights": centred(streams_of[3], (QUERIES, H, K), 0.1, 0.59765625, ((0, 128),)),
    }


def reference(inputs, values, slots, weights):
    flat_slots = slots.reshape(QUERIES, H * K).astype(jnp.int32)
    flat_weights = weights.reshape(QUERIES, H * K)

    def row_sum(pair):
        row_slots, row_weights = pair
        picked = jnp.take(values, row_slots, axis=0)
        return jnp.dot(row_weights[None, :], picked, preferred_element_type=jnp.float32)[0]

    memory = lax.map(row_sum, (flat_slots, flat_weights))
    return (inputs.astype(jnp.float32) + memory).astype(jnp.bfloat16)
```

```python
import jax
import jax.numpy as jnp
from jax import lax
from jax.experimental import pallas as pl
from jax.experimental.pallas import tpu as pltpu
from jax.sharding import Mesh, PartitionSpec as P

AXES = ("y", "core", "z", "x")
CHIPS = ("x", "z", "y")
GROUP = ("core", *CHIPS)
LANES = 128
MIB = 1024 * 1024


def request_kernel(
    owners, cap, slots_hbm, weights_hbm, values_hbm, out_ref, slots_ref, weights_ref, sems
):
    slot_dev = values_hbm.shape[0]
    copies = [
        pltpu.make_async_copy(slots_hbm, slots_ref, sems.at[0]),
        pltpu.make_async_copy(weights_hbm, weights_ref, sems.at[1]),
    ]
    for copy in copies:
        copy.start()
    for copy in copies:
        copy.wait()
    heads = slots_ref.shape[1]
    slots = slots_ref[0]
    weights = weights_ref[0].astype(jnp.float32)
    slots = jnp.concatenate([slots[h : h + 1] for h in range(heads)], axis=1)
    weights = jnp.concatenate([weights[h : h + 1] for h in range(heads)], axis=1)
    picks = slots.shape[1]
    owner = slots // slot_dev
    row = slots - owner * slot_dev
    low = row % 32
    high = row - low
    xs, zs, ys = (lax.axis_size(axis) for axis in CHIPS)
    y, core = owner // (2 * zs * xs), owner // (zs * xs) % 2
    z, x = owner // xs % zs, owner % xs
    owner = ((core * xs + x) * zs + z) * ys + y
    mine = owner == lax.broadcasted_iota(jnp.int32, (owners, picks), 0)
    before = lax.broadcasted_iota(jnp.int32, (picks, picks), 0) < lax.broadcasted_iota(
        jnp.int32, (picks, picks), 1
    )
    marks = jnp.where(mine, 1.0, 0.0).astype(jnp.bfloat16)
    earlier = jnp.dot(
        marks,
        jnp.where(before, 1.0, 0.0).astype(jnp.bfloat16),
        preferred_element_type=jnp.float32,
    )
    rank = jnp.sum(jnp.where(mine, earlier, 0.0), axis=0, keepdims=True).astype(jnp.int32)
    lane = lax.broadcasted_iota(jnp.int32, (LANES, picks), 0) - rank
    fields = jnp.where(
        lane == 0,
        high.astype(jnp.float32),
        jnp.where(
            lane == cap, low.astype(jnp.float32), jnp.where(lane == 2 * cap, weights, 0.0)
        ),
    )
    out_ref[...] = lax.dot_general(
        marks,
        fields.astype(jnp.bfloat16),
        (((1,), (1,)), ((), ())),
        preferred_element_type=jnp.float32,
    )


def half_kernel(cap, chunk, other, got_ref, slab_ref, out_ref, table):
    slot_dev, width = slab_ref.shape
    sources = got_ref.shape[0]
    core = lax.axis_index("core")
    core = 1 - core if other else core
    group = 16
    for n in range(sources // group):
        got = got_ref[pl.ds(n * group, group)]

        def spread(lane):
            return jnp.broadcast_to(got[:, lane : lane + 1], (group, LANES))

        rows = [spread(c) + spread(cap + c) for c in range(cap)]
        scales = [spread(2 * cap + c) for c in range(cap)]
        scales = [
            sum(jnp.where(rows[c] == rows[d], scales[d], 0.0) for d in range(cap)).astype(
                jnp.bfloat16
            )
            for c in range(cap)
        ]
        rows = [row.astype(jnp.int32).astype(jnp.int16) for row in rows]
        lane = lax.broadcasted_iota(jnp.int32, (group, LANES), 1)
        for k in range(slot_dev // LANES):
            at = (lane + k * LANES).astype(jnp.int16)
            weight = jnp.zeros((group, LANES), jnp.bfloat16)
            for c in range(cap):
                weight = jnp.where(at == rows[c], scales[c], weight)
            table[pl.ds(n * group, group), pl.ds(k * LANES, LANES)] = weight
    parts = chunk // LANES
    for n in range(width // 2 // chunk):
        columns = pl.ds(pl.multiple_of(core * (width // 2) + n * chunk, chunk), chunk)
        summed = jnp.dot(table[...], slab_ref[:, columns], preferred_element_type=jnp.float32)
        summed = summed.astype(out_ref.dtype)
        out_ref[:, pl.ds(n * parts, parts), :] = summed.reshape(sources, parts, LANES)


def add_kernel(got_ref, kept_ref, out_ref):
    out_ref[...] = (got_ref[...].astype(jnp.float32) + kept_ref[...]).astype(out_ref.dtype)


def sum_kernel(got_ref, inputs_ref, out_ref):
    sources, tiles, _ = got_ref.shape
    chips = sources // 2
    memory = jnp.concatenate(
        [
            jnp.sum(got_ref[pl.ds(core * chips, chips)].astype(jnp.float32), axis=0)
            for core in range(2)
        ],
        axis=0,
    )
    for j in range(2 * tiles):
        part = pl.ds(j * LANES, LANES)
        out_ref[:, part] = (inputs_ref[:, part].astype(jnp.float32) + memory[j : j + 1]).astype(
            jnp.bfloat16
        )


def body(inputs, values, slots, weights):
    owners = lax.axis_size(AXES)
    slot_dev, width = values.shape
    cap = 4 * slots.size // owners
    tiles = width // LANES
    chunk = 2048
    vmem = pl.BlockSpec(memory_space=pltpu.VMEM)
    hbm = pl.BlockSpec(memory_space=pltpu.HBM)

    def call(kernel, shapes, specs, name, scratch=()):
        return pl.pallas_call(
            kernel,
            out_shape=[pltpu.VMEM(*shape) for shape in shapes],
            in_specs=specs,
            out_specs=[vmem] * len(shapes),
            scratch_shapes=scratch,
            compiler_params=pltpu.CompilerParams(vmem_limit_bytes=24 * MIB),
            name=name,
        )

    constrain = pltpu.with_memory_space_constraint
    (packed,) = call(
        lambda *refs: request_kernel(owners, cap, *refs),
        [((owners, LANES), jnp.float32)],
        [hbm] * 3,
        "request",
        [
            pltpu.VMEM(slots.shape, slots.dtype),
            pltpu.VMEM(weights.shape, weights.dtype),
            pltpu.SemaphoreType.DMA((2,)),
        ],
    )(*[constrain(array, pltpu.HBM) for array in (slots, weights, values)])
    got = lax.all_to_all(
        packed.reshape(owners, 1, LANES), GROUP, split_axis=0, concat_axis=0, tiled=True
    ).reshape(owners, LANES)
    half = (owners, tiles // 2, LANES)
    slab = constrain(values, pltpu.VMEM)
    other, own = [
        call(
            lambda *refs, other=other: half_kernel(cap, chunk, other, *refs),
            [(half, jnp.bfloat16 if other else jnp.float32)],
            [vmem] * 2,
            "other_half" if other else "own_half",
            [pltpu.VMEM((owners, slot_dev), jnp.bfloat16)],
        )(got, slab)[0]
        for other in (True, False)
    ]
    swapped = lax.ppermute(other, "core", [(0, 1), (1, 0)])
    (partials,) = call(add_kernel, [(half, jnp.bfloat16)], [vmem] * 2, "add")(swapped, own)
    returned = lax.all_to_all(partials, GROUP, split_axis=0, concat_axis=0, tiled=True)
    return pl.pallas_call(
        sum_kernel,
        out_shape=jax.ShapeDtypeStruct(inputs.shape, jnp.bfloat16),
        in_specs=[vmem] * 2,
        out_specs=vmem,
        compiler_params=pltpu.CompilerParams(vmem_limit_bytes=24 * MIB),
        name="sum",
    )(returned, inputs)


def solution(mesh):
    hst, chip = mesh.devices.shape
    mesh = Mesh(mesh.devices.reshape(hst // 2, 2, 4, chip // 4), AXES)
    in_specs = (P(AXES, None), P(AXES, None), P(AXES, None, None), P(AXES, None, None))
    return jax.shard_map(
        body, mesh=mesh, in_specs=in_specs, out_specs=P(AXES, None), check_vma=False
    )
```

```python
import jax
import jax.numpy as jnp
from jax import lax
from jax.experimental import pallas as pl
from jax.experimental.pallas import tpu as pltpu
from jax.sharding import Mesh, PartitionSpec as P

AXES = ("y", "core", "z", "x")
CHIPS = ("x", "z", "y")
GROUP = ("core", *CHIPS)
LANES = 128
MIB = 1024 * 1024


def request_kernel(
    owners, cap, slots_hbm, weights_hbm, values_hbm, out_ref, slots_ref, weights_ref, sems
):
    slot_dev = values_hbm.shape[0]
    copies = [
        pltpu.make_async_copy(slots_hbm, slots_ref, sems.at[0]),
        pltpu.make_async_copy(weights_hbm, weights_ref, sems.at[1]),
    ]
    for copy in copies:
        copy.start()
    for copy in copies:
        copy.wait()
    heads = slots_ref.shape[1]
    slots = slots_ref[0]
    weights = weights_ref[0].astype(jnp.float32)
    slots = jnp.concatenate([slots[h : h + 1] for h in range(heads)], axis=1)
    weights = jnp.concatenate([weights[h : h + 1] for h in range(heads)], axis=1)
    picks = slots.shape[1]
    owner = slots // slot_dev
    row = slots - owner * slot_dev
    low = row % 32
    high = row - low
    xs, zs, ys = (lax.axis_size(axis) for axis in CHIPS)
    y, core = owner // (2 * zs * xs), owner // (zs * xs) % 2
    z, x = owner // xs % zs, owner % xs
    owner = ((core * xs + x) * zs + z) * ys + y
    mine = owner == lax.broadcasted_iota(jnp.int32, (owners, picks), 0)
    before = lax.broadcasted_iota(jnp.int32, (picks, picks), 0) < lax.broadcasted_iota(
        jnp.int32, (picks, picks), 1
    )
    marks = jnp.where(mine, 1.0, 0.0).astype(jnp.bfloat16)
    earlier = jnp.dot(
        marks,
        jnp.where(before, 1.0, 0.0).astype(jnp.bfloat16),
        preferred_element_type=jnp.float32,
    )
    rank = jnp.sum(jnp.where(mine, earlier, 0.0), axis=0, keepdims=True).astype(jnp.int32)
    lane = lax.broadcasted_iota(jnp.int32, (LANES, picks), 0) - rank
    fields = jnp.where(
        lane == 0,
        high.astype(jnp.float32),
        jnp.where(
            lane == cap, low.astype(jnp.float32), jnp.where(lane == 2 * cap, weights, 0.0)
        ),
    )
    out_ref[...] = lax.dot_general(
        marks,
        fields.astype(jnp.bfloat16),
        (((1,), (1,)), ((), ())),
        preferred_element_type=jnp.float32,
    )


def half_kernel(cap, chunk, other, got_ref, slab_ref, out_ref, table):
    slot_dev, width = slab_ref.shape
    sources = got_ref.shape[0]
    core = lax.axis_index("core")
    core = 1 - core if other else core
    group = 16
    for n in range(sources // group):
        got = got_ref[pl.ds(n * group, group)]

        def spread(lane):
            return jnp.broadcast_to(got[:, lane : lane + 1], (group, LANES))

        rows = [spread(c) + spread(cap + c) for c in range(cap)]
        scales = [spread(2 * cap + c) for c in range(cap)]
        scales = [
            sum(jnp.where(rows[c] == rows[d], scales[d], 0.0) for d in range(cap)).astype(
                jnp.bfloat16
            )
            for c in range(cap)
        ]
        rows = [row.astype(jnp.int32).astype(jnp.int16) for row in rows]
        lane = lax.broadcasted_iota(jnp.int32, (group, LANES), 1)
        for k in range(slot_dev // LANES):
            at = (lane + k * LANES).astype(jnp.int16)
            weight = jnp.zeros((group, LANES), jnp.bfloat16)
            for c in range(cap):
                weight = jnp.where(at == rows[c], scales[c], weight)
            table[pl.ds(n * group, group), pl.ds(k * LANES, LANES)] = weight
    parts = chunk // LANES
    for n in range(width // 2 // chunk):
        columns = pl.ds(pl.multiple_of(core * (width // 2) + n * chunk, chunk), chunk)
        summed = jnp.dot(table[...], slab_ref[:, columns], preferred_element_type=jnp.float32)
        summed = summed.astype(out_ref.dtype)
        out_ref[:, pl.ds(n * parts, parts), :] = summed.reshape(sources, parts, LANES)


def add_kernel(got_ref, kept_ref, out_ref):
    out_ref[...] = (got_ref[...].astype(jnp.float32) + kept_ref[...]).astype(out_ref.dtype)


def sum_kernel(got_ref, inputs_ref, out_ref):
    sources, tiles, _ = got_ref.shape
    chips = sources // 2
    memory = jnp.concatenate(
        [
            sum(
                jnp.sum(got_ref[pl.ds(core * chips + n, 8)].astype(jnp.float32), axis=0)
                for n in range(0, chips, 8)
            )
            for core in range(2)
        ],
        axis=0,
    )
    memory = memory.reshape(1, 2 * tiles * LANES)
    out_ref[...] = (inputs_ref[...].astype(jnp.float32) + memory).astype(jnp.bfloat16)


def body(inputs, values, slots, weights):
    owners = lax.axis_size(AXES)
    slot_dev, width = values.shape
    cap = 4 * slots.size // owners
    tiles = width // LANES
    chunk = 2048
    vmem = pl.BlockSpec(memory_space=pltpu.VMEM)
    hbm = pl.BlockSpec(memory_space=pltpu.HBM)

    def call(kernel, shapes, specs, name, scratch=()):
        return pl.pallas_call(
            kernel,
            out_shape=[pltpu.VMEM(*shape) for shape in shapes],
            in_specs=specs,
            out_specs=[vmem] * len(shapes),
            scratch_shapes=scratch,
            compiler_params=pltpu.CompilerParams(vmem_limit_bytes=24 * MIB),
            name=name,
        )

    constrain = pltpu.with_memory_space_constraint
    (packed,) = call(
        lambda *refs: request_kernel(owners, cap, *refs),
        [((owners, LANES), jnp.float32)],
        [hbm] * 3,
        "request",
        [
            pltpu.VMEM(slots.shape, slots.dtype),
            pltpu.VMEM(weights.shape, weights.dtype),
            pltpu.SemaphoreType.DMA((2,)),
        ],
    )(*[constrain(array, pltpu.HBM) for array in (slots, weights, values)])
    got = lax.all_to_all(
        packed.reshape(owners, 1, LANES), GROUP, split_axis=0, concat_axis=0, tiled=True
    ).reshape(owners, LANES)
    half = (owners, tiles // 2, LANES)
    slab = constrain(values, pltpu.VMEM)
    other, own = [
        call(
            lambda *refs, other=other: half_kernel(cap, chunk, other, *refs),
            [(half, jnp.bfloat16 if other else jnp.float32)],
            [vmem] * 2,
            "other_half" if other else "own_half",
            [pltpu.VMEM((owners, slot_dev), jnp.bfloat16)],
        )(got, slab)[0]
        for other in (True, False)
    ]
    swapped = lax.ppermute(other, "core", [(0, 1), (1, 0)])
    (partials,) = call(add_kernel, [(half, jnp.bfloat16)], [vmem] * 2, "add")(swapped, own)
    returned = lax.all_to_all(partials, GROUP, split_axis=0, concat_axis=0, tiled=True)
    return pl.pallas_call(
        sum_kernel,
        out_shape=jax.ShapeDtypeStruct(inputs.shape, jnp.bfloat16),
        in_specs=[vmem] * 2,
        out_specs=vmem,
        compiler_params=pltpu.CompilerParams(vmem_limit_bytes=24 * MIB),
        name="sum",
    )(returned, inputs)


def solution(mesh):
    hst, chip = mesh.devices.shape
    mesh = Mesh(mesh.devices.reshape(hst // 2, 2, 4, chip // 4), AXES)
    in_specs = (P(AXES, None), P(AXES, None), P(AXES, None, None), P(AXES, None, None))
    return jax.shard_map(
        body, mesh=mesh, in_specs=in_specs, out_specs=P(AXES, None), check_vma=False
    )
```

```python
import jax
import jax.numpy as jnp
from jax import lax
from jax.experimental import pallas as pl
from jax.experimental.pallas import tpu as pltpu
from jax.sharding import Mesh, PartitionSpec as P

AXES = ("y", "core", "z", "x")
CHIPS = ("x", "z", "y")
GROUP = ("core", *CHIPS)
LANES = 128
MIB = 1024 * 1024


def request_kernel(
    owners, cap, slots_hbm, weights_hbm, values_hbm, out_ref, slots_ref, weights_ref, sems
):
    slot_dev = values_hbm.shape[0]
    copies = [
        pltpu.make_async_copy(slots_hbm, slots_ref, sems.at[0]),
        pltpu.make_async_copy(weights_hbm, weights_ref, sems.at[1]),
    ]
    for copy in copies:
        copy.start()
    for copy in copies:
        copy.wait()
    heads = slots_ref.shape[1]
    slots = slots_ref[0]
    weights = weights_ref[0].astype(jnp.float32)
    slots = jnp.concatenate([slots[h : h + 1] for h in range(heads)], axis=1)
    weights = jnp.concatenate([weights[h : h + 1] for h in range(heads)], axis=1)
    picks = slots.shape[1]
    owner = slots // slot_dev
    row = slots - owner * slot_dev
    low = row % 32
    high = row - low
    xs, zs, ys = (lax.axis_size(axis) for axis in CHIPS)
    y, core = owner // (2 * zs * xs), owner // (zs * xs) % 2
    z, x = owner // xs % zs, owner % xs
    owner = ((core * xs + x) * zs + z) * ys + y
    mine = owner == lax.broadcasted_iota(jnp.int32, (owners, picks), 0)
    before = lax.broadcasted_iota(jnp.int32, (picks, picks), 0) < lax.broadcasted_iota(
        jnp.int32, (picks, picks), 1
    )
    marks = jnp.where(mine, 1.0, 0.0).astype(jnp.bfloat16)
    earlier = jnp.dot(
        marks,
        jnp.where(before, 1.0, 0.0).astype(jnp.bfloat16),
        preferred_element_type=jnp.float32,
    )
    rank = jnp.sum(jnp.where(mine, earlier, 0.0), axis=0, keepdims=True).astype(jnp.int32)
    lane = lax.broadcasted_iota(jnp.int32, (LANES, picks), 0) - rank
    fields = jnp.where(
        lane == 0,
        high.astype(jnp.float32),
        jnp.where(
            lane == cap, low.astype(jnp.float32), jnp.where(lane == 2 * cap, weights, 0.0)
        ),
    )
    out_ref[...] = lax.dot_general(
        marks,
        fields.astype(jnp.bfloat16),
        (((1,), (1,)), ((), ())),
        preferred_element_type=jnp.float32,
    )


def half_kernel(cap, chunk, other, got_ref, slab_ref, out_ref, table):
    slot_dev, width = slab_ref.shape
    sources = got_ref.shape[0]
    core = lax.axis_index("core")
    core = 1 - core if other else core
    group = 16
    for n in range(sources // group):
        got = got_ref[pl.ds(n * group, group)]

        def spread(lane):
            return jnp.broadcast_to(got[:, lane : lane + 1], (group, LANES))

        rows = [spread(c) + spread(cap + c) for c in range(cap)]
        scales = [spread(2 * cap + c) for c in range(cap)]
        same = {(c, d): rows[c] == rows[d] for d in range(cap) for c in range(d)}
        totals = list(scales)
        for (c, d), match in same.items():
            totals[c] = totals[c] + jnp.where(match, scales[d], 0.0)
            totals[d] = totals[d] + jnp.where(match, scales[c], 0.0)
        scales = [total.astype(jnp.bfloat16) for total in totals]
        rows = [row.astype(jnp.int32).astype(jnp.int16) for row in rows]
        lane = lax.broadcasted_iota(jnp.int32, (group, LANES), 1)
        for k in range(slot_dev // LANES):
            at = (lane + k * LANES).astype(jnp.int16)
            weight = jnp.zeros((group, LANES), jnp.bfloat16)
            for c in range(cap):
                weight = jnp.where(at == rows[c], scales[c], weight)
            table[pl.ds(n * group, group), pl.ds(k * LANES, LANES)] = weight
    parts = chunk // LANES
    for n in range(width // 2 // chunk):
        columns = pl.ds(pl.multiple_of(core * (width // 2) + n * chunk, chunk), chunk)
        summed = jnp.dot(table[...], slab_ref[:, columns], preferred_element_type=jnp.float32)
        summed = summed.astype(out_ref.dtype)
        out_ref[:, pl.ds(n * parts, parts), :] = summed.reshape(sources, parts, LANES)


def add_kernel(got_ref, kept_ref, out_ref):
    out_ref[...] = (got_ref[...].astype(jnp.float32) + kept_ref[...]).astype(out_ref.dtype)


def sum_kernel(got_ref, inputs_ref, out_ref):
    sources, tiles, _ = got_ref.shape
    chips = sources // 2
    memory = jnp.concatenate(
        [
            sum(
                jnp.sum(got_ref[pl.ds(core * chips + n, 8)].astype(jnp.float32), axis=0)
                for n in range(0, chips, 8)
            )
            for core in range(2)
        ],
        axis=0,
    )
    memory = memory.reshape(1, 2 * tiles * LANES)
    out_ref[...] = (inputs_ref[...].astype(jnp.float32) + memory).astype(jnp.bfloat16)


def body(inputs, values, slots, weights):
    owners = lax.axis_size(AXES)
    slot_dev, width = values.shape
    cap = 4 * slots.size // owners
    tiles = width // LANES
    chunk = 2048
    vmem = pl.BlockSpec(memory_space=pltpu.VMEM)
    hbm = pl.BlockSpec(memory_space=pltpu.HBM)

    def call(kernel, shapes, specs, name, scratch=()):
        return pl.pallas_call(
            kernel,
            out_shape=[pltpu.VMEM(*shape) for shape in shapes],
            in_specs=specs,
            out_specs=[vmem] * len(shapes),
            scratch_shapes=scratch,
            compiler_params=pltpu.CompilerParams(vmem_limit_bytes=24 * MIB),
            name=name,
        )

    constrain = pltpu.with_memory_space_constraint
    (packed,) = call(
        lambda *refs: request_kernel(owners, cap, *refs),
        [((owners, LANES), jnp.float32)],
        [hbm] * 3,
        "request",
        [
            pltpu.VMEM(slots.shape, slots.dtype),
            pltpu.VMEM(weights.shape, weights.dtype),
            pltpu.SemaphoreType.DMA((2,)),
        ],
    )(*[constrain(array, pltpu.HBM) for array in (slots, weights, values)])
    got = lax.all_to_all(
        packed.reshape(owners, 1, LANES), GROUP, split_axis=0, concat_axis=0, tiled=True
    ).reshape(owners, LANES)
    half = (owners, tiles // 2, LANES)
    slab = constrain(values, pltpu.VMEM)
    other, own = [
        call(
            lambda *refs, other=other: half_kernel(cap, chunk, other, *refs),
            [(half, jnp.bfloat16 if other else jnp.float32)],
            [vmem] * 2,
            "other_half" if other else "own_half",
            [pltpu.VMEM((owners, slot_dev), jnp.bfloat16)],
        )(got, slab)[0]
        for other in (True, False)
    ]
    swapped = lax.ppermute(other, "core", [(0, 1), (1, 0)])
    (partials,) = call(add_kernel, [(half, jnp.bfloat16)], [vmem] * 2, "add")(swapped, own)
    returned = lax.all_to_all(partials, GROUP, split_axis=0, concat_axis=0, tiled=True)
    return pl.pallas_call(
        sum_kernel,
        out_shape=jax.ShapeDtypeStruct(inputs.shape, jnp.bfloat16),
        in_specs=[vmem] * 2,
        out_specs=vmem,
        compiler_params=pltpu.CompilerParams(vmem_limit_bytes=24 * MIB),
        name="sum",
    )(returned, inputs)


def solution(mesh):
    hst, chip = mesh.devices.shape
    mesh = Mesh(mesh.devices.reshape(hst // 2, 2, 4, chip // 4), AXES)
    in_specs = (P(AXES, None), P(AXES, None), P(AXES, None, None), P(AXES, None, None))
    return jax.shard_map(
        body, mesh=mesh, in_specs=in_specs, out_specs=P(AXES, None), check_vma=False
    )
```

```python
import jax
import jax.numpy as jnp
from jax import lax
from jax.experimental import pallas as pl
from jax.experimental.pallas import tpu as pltpu
from jax.sharding import Mesh, PartitionSpec as P

AXES = ("y", "core", "z", "x")
CHIPS = ("x", "z", "y")
GROUP = ("core", *CHIPS)
LANES = 128
MIB = 1024 * 1024


def request_kernel(
    owners, cap, slots_hbm, weights_hbm, values_hbm, out_ref, slots_ref, weights_ref, sems
):
    slot_dev = values_hbm.shape[0]
    copies = [
        pltpu.make_async_copy(slots_hbm, slots_ref, sems.at[0]),
        pltpu.make_async_copy(weights_hbm, weights_ref, sems.at[1]),
    ]
    for copy in copies:
        copy.start()
    for copy in copies:
        copy.wait()
    heads = slots_ref.shape[1]
    slots = slots_ref[0]
    weights = weights_ref[0].astype(jnp.float32)
    slots = jnp.concatenate([slots[h : h + 1] for h in range(heads)], axis=1)
    weights = jnp.concatenate([weights[h : h + 1] for h in range(heads)], axis=1)
    picks = slots.shape[1]
    owner = slots // slot_dev
    row = slots - owner * slot_dev
    low = row % 32
    high = row - low
    xs, zs, ys = (lax.axis_size(axis) for axis in CHIPS)
    y, core = owner // (2 * zs * xs), owner // (zs * xs) % 2
    z, x = owner // xs % zs, owner % xs
    owner = ((core * xs + x) * zs + z) * ys + y
    mine = owner == lax.broadcasted_iota(jnp.int32, (owners, picks), 0)
    before = lax.broadcasted_iota(jnp.int32, (picks, picks), 0) < lax.broadcasted_iota(
        jnp.int32, (picks, picks), 1
    )
    marks = jnp.where(mine, 1.0, 0.0).astype(jnp.bfloat16)
    earlier = jnp.dot(
        marks,
        jnp.where(before, 1.0, 0.0).astype(jnp.bfloat16),
        preferred_element_type=jnp.float32,
    )
    rank = jnp.sum(jnp.where(mine, earlier, 0.0), axis=0, keepdims=True).astype(jnp.int32)
    lane = lax.broadcasted_iota(jnp.int32, (LANES, picks), 0) - rank
    fields = jnp.where(
        lane == 0,
        high.astype(jnp.float32),
        jnp.where(
            lane == cap, low.astype(jnp.float32), jnp.where(lane == 2 * cap, weights, 0.0)
        ),
    )
    out_ref[...] = lax.dot_general(
        marks,
        fields.astype(jnp.bfloat16),
        (((1,), (1,)), ((), ())),
        preferred_element_type=jnp.float32,
    )


def half_kernel(cap, chunk, other, got_ref, slab_ref, out_ref, table):
    slot_dev, width = slab_ref.shape
    sources = got_ref.shape[0]
    core = lax.axis_index("core")
    core = 1 - core if other else core
    field = lax.broadcasted_iota(jnp.int32, (LANES, 2 * cap * LANES), 0)
    block = lax.broadcasted_iota(jnp.int32, (LANES, 2 * cap * LANES), 1) // LANES
    wanted = (field == block + cap) | ((field == block) & (block < cap))
    spread = jnp.dot(
        got_ref[...].astype(jnp.bfloat16),
        jnp.where(wanted, 1.0, 0.0).astype(jnp.bfloat16),
        preferred_element_type=jnp.float32,
    )
    group = 16
    for n in range(sources // group):
        blocks = [
            spread[n * group : (n + 1) * group, c * LANES : (c + 1) * LANES]
            for c in range(2 * cap)
        ]
        rows, scales = blocks[:cap], blocks[cap:]
        scales = [
            sum(jnp.where(rows[c] == rows[d], scales[d], 0.0) for d in range(cap)).astype(
                jnp.bfloat16
            )
            for c in range(cap)
        ]
        rows = [row.astype(jnp.int32).astype(jnp.int16) for row in rows]
        lane = lax.broadcasted_iota(jnp.int32, (group, LANES), 1)
        for k in range(slot_dev // LANES):
            at = (lane + k * LANES).astype(jnp.int16)
            weight = jnp.zeros((group, LANES), jnp.bfloat16)
            for c in range(cap):
                weight = jnp.where(at == rows[c], scales[c], weight)
            table[pl.ds(n * group, group), pl.ds(k * LANES, LANES)] = weight
    parts = chunk // LANES
    for n in range(width // 2 // chunk):
        columns = pl.ds(pl.multiple_of(core * (width // 2) + n * chunk, chunk), chunk)
        summed = jnp.dot(table[...], slab_ref[:, columns], preferred_element_type=jnp.float32)
        summed = summed.astype(out_ref.dtype)
        out_ref[:, pl.ds(n * parts, parts), :] = summed.reshape(sources, parts, LANES)


def add_kernel(got_ref, kept_ref, out_ref):
    out_ref[...] = (got_ref[...].astype(jnp.float32) + kept_ref[...]).astype(out_ref.dtype)


def sum_kernel(got_ref, inputs_ref, out_ref):
    sources, tiles, _ = got_ref.shape
    chips = sources // 2
    memory = jnp.concatenate(
        [
            sum(
                jnp.sum(got_ref[pl.ds(core * chips + n, 8)].astype(jnp.float32), axis=0)
                for n in range(0, chips, 8)
            )
            for core in range(2)
        ],
        axis=0,
    )
    memory = memory.reshape(1, 2 * tiles * LANES)
    out_ref[...] = (inputs_ref[...].astype(jnp.float32) + memory).astype(jnp.bfloat16)


def body(inputs, values, slots, weights):
    owners = lax.axis_size(AXES)
    slot_dev, width = values.shape
    cap = 4 * slots.size // owners
    tiles = width // LANES
    chunk = 2048
    vmem = pl.BlockSpec(memory_space=pltpu.VMEM)
    hbm = pl.BlockSpec(memory_space=pltpu.HBM)

    def call(kernel, shapes, specs, name, scratch=()):
        return pl.pallas_call(
            kernel,
            out_shape=[pltpu.VMEM(*shape) for shape in shapes],
            in_specs=specs,
            out_specs=[vmem] * len(shapes),
            scratch_shapes=scratch,
            compiler_params=pltpu.CompilerParams(vmem_limit_bytes=24 * MIB),
            name=name,
        )

    constrain = pltpu.with_memory_space_constraint
    (packed,) = call(
        lambda *refs: request_kernel(owners, cap, *refs),
        [((owners, LANES), jnp.float32)],
        [hbm] * 3,
        "request",
        [
            pltpu.VMEM(slots.shape, slots.dtype),
            pltpu.VMEM(weights.shape, weights.dtype),
            pltpu.SemaphoreType.DMA((2,)),
        ],
    )(*[constrain(array, pltpu.HBM) for array in (slots, weights, values)])
    got = lax.all_to_all(
        packed.reshape(owners, 1, LANES), GROUP, split_axis=0, concat_axis=0, tiled=True
    ).reshape(owners, LANES)
    half = (owners, tiles // 2, LANES)
    slab = constrain(values, pltpu.VMEM)
    other, own = [
        call(
            lambda *refs, other=other: half_kernel(cap, chunk, other, *refs),
            [(half, jnp.bfloat16 if other else jnp.float32)],
            [vmem] * 2,
            "other_half" if other else "own_half",
            [pltpu.VMEM((owners, slot_dev), jnp.bfloat16)],
        )(got, slab)[0]
        for other in (True, False)
    ]
    swapped = lax.ppermute(other, "core", [(0, 1), (1, 0)])
    (partials,) = call(add_kernel, [(half, jnp.bfloat16)], [vmem] * 2, "add")(swapped, own)
    returned = lax.all_to_all(partials, GROUP, split_axis=0, concat_axis=0, tiled=True)
    return pl.pallas_call(
        sum_kernel,
        out_shape=jax.ShapeDtypeStruct(inputs.shape, jnp.bfloat16),
        in_specs=[vmem] * 2,
        out_specs=vmem,
        compiler_params=pltpu.CompilerParams(vmem_limit_bytes=24 * MIB),
        name="sum",
    )(returned, inputs)


def solution(mesh):
    hst, chip = mesh.devices.shape
    mesh = Mesh(mesh.devices.reshape(hst // 2, 2, 4, chip // 4), AXES)
    in_specs = (P(AXES, None), P(AXES, None), P(AXES, None, None), P(AXES, None, None))
    return jax.shard_map(
        body, mesh=mesh, in_specs=in_specs, out_specs=P(AXES, None), check_vma=False
    )
```

```python
import jax
import jax.numpy as jnp
from jax import lax
from jax.experimental import pallas as pl
from jax.experimental.pallas import tpu as pltpu
from jax.sharding import Mesh, PartitionSpec as P

AXES = ("y", "core", "z", "x")
CHIPS = ("x", "z", "y")
GROUP = ("core", *CHIPS)
LANES = 128
MIB = 1024 * 1024


def request_kernel(
    owners, cap, slots_hbm, weights_hbm, values_hbm, out_ref, slots_ref, weights_ref, sems
):
    slot_dev = values_hbm.shape[0]
    copies = [
        pltpu.make_async_copy(slots_hbm, slots_ref, sems.at[0]),
        pltpu.make_async_copy(weights_hbm, weights_ref, sems.at[1]),
    ]
    for copy in copies:
        copy.start()
    for copy in copies:
        copy.wait()
    heads = slots_ref.shape[1]
    slots = slots_ref[0]
    weights = weights_ref[0].astype(jnp.float32)
    slots = jnp.concatenate([slots[h : h + 1] for h in range(heads)], axis=1)
    weights = jnp.concatenate([weights[h : h + 1] for h in range(heads)], axis=1)
    picks = slots.shape[1]
    owner = slots // slot_dev
    row = slots - owner * slot_dev
    low = row % 32
    high = row - low
    xs, zs, ys = (lax.axis_size(axis) for axis in CHIPS)
    y, core = owner // (2 * zs * xs), owner // (zs * xs) % 2
    z, x = owner // xs % zs, owner % xs
    owner = ((core * xs + x) * zs + z) * ys + y
    mine = owner == lax.broadcasted_iota(jnp.int32, (owners, picks), 0)
    before = lax.broadcasted_iota(jnp.int32, (picks, picks), 0) < lax.broadcasted_iota(
        jnp.int32, (picks, picks), 1
    )
    marks = jnp.where(mine, 1.0, 0.0).astype(jnp.bfloat16)
    earlier = jnp.dot(
        marks,
        jnp.where(before, 1.0, 0.0).astype(jnp.bfloat16),
        preferred_element_type=jnp.float32,
    )
    rank = jnp.sum(jnp.where(mine, earlier, 0.0), axis=0, keepdims=True).astype(jnp.int32)
    lane = lax.broadcasted_iota(jnp.int32, (LANES, picks), 0) - rank
    fields = jnp.where(
        lane == 0,
        high.astype(jnp.float32),
        jnp.where(
            lane == cap, low.astype(jnp.float32), jnp.where(lane == 2 * cap, weights, 0.0)
        ),
    )
    out_ref[...] = lax.dot_general(
        marks,
        fields.astype(jnp.bfloat16),
        (((1,), (1,)), ((), ())),
        preferred_element_type=jnp.float32,
    )


def half_kernel(cap, chunk, other, got_ref, slab_ref, out_ref, table):
    slot_dev, width = slab_ref.shape
    sources = got_ref.shape[0]
    core = lax.axis_index("core")
    core = 1 - core if other else core
    field = lax.broadcasted_iota(jnp.int32, (LANES, 2 * cap * LANES), 0)
    block = lax.broadcasted_iota(jnp.int32, (LANES, 2 * cap * LANES), 1) // LANES
    wanted = (field == block + cap) | ((field == block) & (block < cap))
    spread = jnp.dot(
        got_ref[...].astype(jnp.bfloat16),
        jnp.where(wanted, 1.0, 0.0).astype(jnp.bfloat16),
        preferred_element_type=jnp.float32,
    )
    group = 16
    for n in range(sources // group):
        blocks = [
            spread[n * group : (n + 1) * group, c * LANES : (c + 1) * LANES]
            for c in range(2 * cap)
        ]
        rows, scales = blocks[:cap], blocks[cap:]
        same = {(c, d): rows[c] == rows[d] for d in range(cap) for c in range(d)}
        totals = list(scales)
        for (c, d), match in same.items():
            totals[c] = totals[c] + jnp.where(match, scales[d], 0.0)
            totals[d] = totals[d] + jnp.where(match, scales[c], 0.0)
        scales = [total.astype(jnp.bfloat16) for total in totals]
        rows = [row.astype(jnp.int32).astype(jnp.int16) for row in rows]
        lane = lax.broadcasted_iota(jnp.int32, (group, LANES), 1)
        for k in range(slot_dev // LANES):
            at = (lane + k * LANES).astype(jnp.int16)
            weight = jnp.zeros((group, LANES), jnp.bfloat16)
            for c in range(cap):
                weight = jnp.where(at == rows[c], scales[c], weight)
            table[pl.ds(n * group, group), pl.ds(k * LANES, LANES)] = weight
    parts = chunk // LANES
    for n in range(width // 2 // chunk):
        columns = pl.ds(pl.multiple_of(core * (width // 2) + n * chunk, chunk), chunk)
        summed = jnp.dot(table[...], slab_ref[:, columns], preferred_element_type=jnp.float32)
        summed = summed.astype(out_ref.dtype)
        out_ref[:, pl.ds(n * parts, parts), :] = summed.reshape(sources, parts, LANES)


def add_kernel(got_ref, kept_ref, out_ref):
    out_ref[...] = (got_ref[...].astype(jnp.float32) + kept_ref[...]).astype(out_ref.dtype)


def sum_kernel(got_ref, inputs_ref, out_ref):
    sources, tiles, _ = got_ref.shape
    chips = sources // 2
    memory = jnp.concatenate(
        [
            sum(
                jnp.sum(got_ref[pl.ds(core * chips + n, 8)].astype(jnp.float32), axis=0)
                for n in range(0, chips, 8)
            )
            for core in range(2)
        ],
        axis=0,
    )
    memory = memory.reshape(1, 2 * tiles * LANES)
    out_ref[...] = (inputs_ref[...].astype(jnp.float32) + memory).astype(jnp.bfloat16)


def body(inputs, values, slots, weights):
    owners = lax.axis_size(AXES)
    slot_dev, width = values.shape
    cap = 4 * slots.size // owners
    tiles = width // LANES
    chunk = 2048
    vmem = pl.BlockSpec(memory_space=pltpu.VMEM)
    hbm = pl.BlockSpec(memory_space=pltpu.HBM)

    def call(kernel, shapes, specs, name, scratch=()):
        return pl.pallas_call(
            kernel,
            out_shape=[pltpu.VMEM(*shape) for shape in shapes],
            in_specs=specs,
            out_specs=[vmem] * len(shapes),
            scratch_shapes=scratch,
            compiler_params=pltpu.CompilerParams(vmem_limit_bytes=24 * MIB),
            name=name,
        )

    constrain = pltpu.with_memory_space_constraint
    (packed,) = call(
        lambda *refs: request_kernel(owners, cap, *refs),
        [((owners, LANES), jnp.float32)],
        [hbm] * 3,
        "request",
        [
            pltpu.VMEM(slots.shape, slots.dtype),
            pltpu.VMEM(weights.shape, weights.dtype),
            pltpu.SemaphoreType.DMA((2,)),
        ],
    )(*[constrain(array, pltpu.HBM) for array in (slots, weights, values)])
    got = lax.all_to_all(
        packed.reshape(owners, 1, LANES), GROUP, split_axis=0, concat_axis=0, tiled=True
    ).reshape(owners, LANES)
    half = (owners, tiles // 2, LANES)
    slab = constrain(values, pltpu.VMEM)
    other, own = [
        call(
            lambda *refs, other=other: half_kernel(cap, chunk, other, *refs),
            [(half, jnp.bfloat16 if other else jnp.float32)],
            [vmem] * 2,
            "other_half" if other else "own_half",
            [pltpu.VMEM((owners, slot_dev), jnp.bfloat16)],
        )(got, slab)[0]
        for other in (True, False)
    ]
    swapped = lax.ppermute(other, "core", [(0, 1), (1, 0)])
    (partials,) = call(add_kernel, [(half, jnp.bfloat16)], [vmem] * 2, "add")(swapped, own)
    returned = lax.all_to_all(partials, GROUP, split_axis=0, concat_axis=0, tiled=True)
    return pl.pallas_call(
        sum_kernel,
        out_shape=jax.ShapeDtypeStruct(inputs.shape, jnp.bfloat16),
        in_specs=[vmem] * 2,
        out_specs=vmem,
        compiler_params=pltpu.CompilerParams(vmem_limit_bytes=24 * MIB),
        name="sum",
    )(returned, inputs)


def solution(mesh):
    hst, chip = mesh.devices.shape
    mesh = Mesh(mesh.devices.reshape(hst // 2, 2, 4, chip // 4), AXES)
    in_specs = (P(AXES, None), P(AXES, None), P(AXES, None, None), P(AXES, None, None))
    return jax.shard_map(
        body, mesh=mesh, in_specs=in_specs, out_specs=P(AXES, None), check_vma=False
    )
```

```python
import jax
import jax.numpy as jnp
from jax import lax
from jax.experimental import pallas as pl
from jax.experimental.pallas import tpu as pltpu
from jax.sharding import Mesh, PartitionSpec as P

AXES = ("y", "core", "z", "x")
CHIPS = ("x", "z", "y")
GROUP = ("core", *CHIPS)
LANES = 128
MIB = 1024 * 1024


def request_kernel(
    owners, cap, slots_hbm, weights_hbm, values_hbm, out_ref, slots_ref, weights_ref, sems
):
    slot_dev = values_hbm.shape[0]
    copies = [
        pltpu.make_async_copy(slots_hbm, slots_ref, sems.at[0]),
        pltpu.make_async_copy(weights_hbm, weights_ref, sems.at[1]),
    ]
    for copy in copies:
        copy.start()
    for copy in copies:
        copy.wait()
    heads = slots_ref.shape[1]
    slots = slots_ref[0]
    weights = weights_ref[0].astype(jnp.float32)
    slots = jnp.concatenate([slots[h : h + 1] for h in range(heads)], axis=1)
    weights = jnp.concatenate([weights[h : h + 1] for h in range(heads)], axis=1)
    picks = slots.shape[1]
    owner = slots // slot_dev
    row = slots - owner * slot_dev
    low = row % 32
    high = row - low
    xs, zs, ys = (lax.axis_size(axis) for axis in CHIPS)
    y, core = owner // (2 * zs * xs), owner // (zs * xs) % 2
    z, x = owner // xs % zs, owner % xs
    owner = ((core * xs + x) * zs + z) * ys + y
    mine = owner == lax.broadcasted_iota(jnp.int32, (owners, picks), 0)
    before = lax.broadcasted_iota(jnp.int32, (picks, picks), 0) < lax.broadcasted_iota(
        jnp.int32, (picks, picks), 1
    )
    marks = jnp.where(mine, 1.0, 0.0).astype(jnp.bfloat16)
    earlier = jnp.dot(
        marks,
        jnp.where(before, 1.0, 0.0).astype(jnp.bfloat16),
        preferred_element_type=jnp.float32,
    )
    rank = jnp.sum(jnp.where(mine, earlier, 0.0), axis=0, keepdims=True).astype(jnp.int32)
    lane = lax.broadcasted_iota(jnp.int32, (LANES, picks), 0) - rank
    fields = jnp.where(
        lane == 0,
        high.astype(jnp.float32),
        jnp.where(
            lane == cap, low.astype(jnp.float32), jnp.where(lane == 2 * cap, weights, 0.0)
        ),
    )
    out_ref[...] = lax.dot_general(
        marks,
        fields.astype(jnp.bfloat16),
        (((1,), (1,)), ((), ())),
        preferred_element_type=jnp.float32,
    )


def half_kernel(cap, chunk, other, got_ref, slab_ref, out_ref, table):
    slot_dev, width = slab_ref.shape
    sources = got_ref.shape[0]
    core = lax.axis_index("core")
    core = 1 - core if other else core
    field = lax.broadcasted_iota(jnp.int32, (LANES, 2 * cap * LANES), 0)
    block = lax.broadcasted_iota(jnp.int32, (LANES, 2 * cap * LANES), 1) // LANES
    wanted = (field == block + cap) | ((field == block) & (block < cap))
    spread = jnp.dot(
        got_ref[...].astype(jnp.bfloat16),
        jnp.where(wanted, 1.0, 0.0).astype(jnp.bfloat16),
        preferred_element_type=jnp.float32,
    )
    group = 32
    lane = lax.broadcasted_iota(jnp.int32, (group, LANES), 1)
    places = [(lane + k).astype(jnp.int16) for k in range(0, slot_dev, LANES)]
    for n in range(sources // group):
        blocks = [
            spread[n * group : (n + 1) * group, c * LANES : (c + 1) * LANES]
            for c in range(2 * cap)
        ]
        rows, scales = blocks[:cap], blocks[cap:]
        same = {(c, d): rows[c] == rows[d] for d in range(cap) for c in range(d)}
        totals = list(scales)
        for (c, d), match in same.items():
            totals[c] = totals[c] + jnp.where(match, scales[d], 0.0)
            totals[d] = totals[d] + jnp.where(match, scales[c], 0.0)
        scales = [total.astype(jnp.bfloat16) for total in totals]
        rows = [row.astype(jnp.int32).astype(jnp.int16) for row in rows]
        for k, at in enumerate(places):
            weight = jnp.zeros((group, LANES), jnp.bfloat16)
            for c in range(cap):
                weight = jnp.where(at == rows[c], scales[c], weight)
            table[pl.ds(n * group, group), pl.ds(k * LANES, LANES)] = weight
    parts = chunk // LANES
    for n in range(width // 2 // chunk):
        columns = pl.ds(pl.multiple_of(core * (width // 2) + n * chunk, chunk), chunk)
        summed = jnp.dot(table[...], slab_ref[:, columns], preferred_element_type=jnp.float32)
        summed = summed.astype(out_ref.dtype)
        out_ref[:, pl.ds(n * parts, parts), :] = summed.reshape(sources, parts, LANES)


def add_kernel(got_ref, kept_ref, out_ref):
    out_ref[...] = (got_ref[...].astype(jnp.float32) + kept_ref[...]).astype(out_ref.dtype)


def sum_kernel(got_ref, inputs_ref, out_ref):
    sources, tiles, _ = got_ref.shape
    chips = sources // 2
    memory = jnp.concatenate(
        [
            sum(
                jnp.sum(got_ref[pl.ds(core * chips + n, 8)].astype(jnp.float32), axis=0)
                for n in range(0, chips, 8)
            )
            for core in range(2)
        ],
        axis=0,
    )
    memory = memory.reshape(1, 2 * tiles * LANES)
    out_ref[...] = (inputs_ref[...].astype(jnp.float32) + memory).astype(jnp.bfloat16)


def body(inputs, values, slots, weights):
    owners = lax.axis_size(AXES)
    slot_dev, width = values.shape
    cap = 4 * slots.size // owners
    tiles = width // LANES
    chunk = 2048
    vmem = pl.BlockSpec(memory_space=pltpu.VMEM)
    hbm = pl.BlockSpec(memory_space=pltpu.HBM)

    def call(kernel, shapes, specs, name, scratch=()):
        return pl.pallas_call(
            kernel,
            out_shape=[pltpu.VMEM(*shape) for shape in shapes],
            in_specs=specs,
            out_specs=[vmem] * len(shapes),
            scratch_shapes=scratch,
            compiler_params=pltpu.CompilerParams(vmem_limit_bytes=24 * MIB),
            name=name,
        )

    constrain = pltpu.with_memory_space_constraint
    (packed,) = call(
        lambda *refs: request_kernel(owners, cap, *refs),
        [((owners, LANES), jnp.float32)],
        [hbm] * 3,
        "request",
        [
            pltpu.VMEM(slots.shape, slots.dtype),
            pltpu.VMEM(weights.shape, weights.dtype),
            pltpu.SemaphoreType.DMA((2,)),
        ],
    )(*[constrain(array, pltpu.HBM) for array in (slots, weights, values)])
    got = lax.all_to_all(
        packed.reshape(owners, 1, LANES), GROUP, split_axis=0, concat_axis=0, tiled=True
    ).reshape(owners, LANES)
    half = (owners, tiles // 2, LANES)
    slab = constrain(values, pltpu.VMEM)
    other, own = [
        call(
            lambda *refs, other=other: half_kernel(cap, chunk, other, *refs),
            [(half, jnp.bfloat16 if other else jnp.float32)],
            [vmem] * 2,
            "other_half" if other else "own_half",
            [pltpu.VMEM((owners, slot_dev), jnp.bfloat16)],
        )(got, slab)[0]
        for other in (True, False)
    ]
    swapped = lax.ppermute(other, "core", [(0, 1), (1, 0)])
    (partials,) = call(add_kernel, [(half, jnp.bfloat16)], [vmem] * 2, "add")(swapped, own)
    returned = lax.all_to_all(partials, GROUP, split_axis=0, concat_axis=0, tiled=True)
    return pl.pallas_call(
        sum_kernel,
        out_shape=jax.ShapeDtypeStruct(inputs.shape, jnp.bfloat16),
        in_specs=[vmem] * 2,
        out_specs=vmem,
        compiler_params=pltpu.CompilerParams(vmem_limit_bytes=24 * MIB),
        name="sum",
    )(returned, inputs)


def solution(mesh):
    hst, chip = mesh.devices.shape
    mesh = Mesh(mesh.devices.reshape(hst // 2, 2, 4, chip // 4), AXES)
    in_specs = (P(AXES, None), P(AXES, None), P(AXES, None, None), P(AXES, None, None))
    return jax.shard_map(
        body, mesh=mesh, in_specs=in_specs, out_specs=P(AXES, None), check_vma=False
    )
```

```python
import jax
import jax.numpy as jnp
from jax import lax
from jax.experimental import pallas as pl
from jax.experimental.pallas import tpu as pltpu
from jax.sharding import Mesh, PartitionSpec as P

AXES = ("y", "core", "z", "x")
CHIPS = ("x", "z", "y")
GROUP = ("core", *CHIPS)
LANES = 128
MIB = 1024 * 1024


def request_kernel(
    owners, cap, slots_hbm, weights_hbm, values_hbm, out_ref, slots_ref, weights_ref, sems
):
    slot_dev = values_hbm.shape[0]
    copies = [
        pltpu.make_async_copy(slots_hbm, slots_ref, sems.at[0]),
        pltpu.make_async_copy(weights_hbm, weights_ref, sems.at[1]),
    ]
    for copy in copies:
        copy.start()
    for copy in copies:
        copy.wait()
    heads = slots_ref.shape[1]
    slots = slots_ref[0]
    weights = weights_ref[0].astype(jnp.float32)
    slots = jnp.concatenate([slots[h : h + 1] for h in range(heads)], axis=1)
    weights = jnp.concatenate([weights[h : h + 1] for h in range(heads)], axis=1)
    picks = slots.shape[1]
    owner = slots // slot_dev
    row = slots - owner * slot_dev
    low = row % 32
    high = row - low
    xs, zs, ys = (lax.axis_size(axis) for axis in CHIPS)
    y, core = owner // (2 * zs * xs), owner // (zs * xs) % 2
    z, x = owner // xs % zs, owner % xs
    owner = ((core * xs + x) * zs + z) * ys + y
    mine = owner == lax.broadcasted_iota(jnp.int32, (owners, picks), 0)
    before = lax.broadcasted_iota(jnp.int32, (picks, picks), 0) < lax.broadcasted_iota(
        jnp.int32, (picks, picks), 1
    )
    marks = jnp.where(mine, 1.0, 0.0).astype(jnp.bfloat16)
    earlier = jnp.dot(
        marks,
        jnp.where(before, 1.0, 0.0).astype(jnp.bfloat16),
        preferred_element_type=jnp.float32,
    )
    rank = jnp.sum(jnp.where(mine, earlier, 0.0), axis=0, keepdims=True).astype(jnp.int32)
    lane = lax.broadcasted_iota(jnp.int32, (LANES, picks), 0) - rank
    fields = jnp.where(
        lane == 0,
        high.astype(jnp.float32),
        jnp.where(
            lane == cap, low.astype(jnp.float32), jnp.where(lane == 2 * cap, weights, 0.0)
        ),
    )
    out_ref[...] = lax.dot_general(
        marks,
        fields.astype(jnp.bfloat16),
        (((1,), (1,)), ((), ())),
        preferred_element_type=jnp.float32,
    )


def half_kernel(cap, chunk, other, got_ref, slab_ref, out_ref, table):
    slot_dev, width = slab_ref.shape
    sources = got_ref.shape[0]
    core = lax.axis_index("core")
    core = 1 - core if other else core
    fields = 4 * cap
    field = lax.broadcasted_iota(jnp.int32, (fields, 2 * cap * LANES), 0)
    block = lax.broadcasted_iota(jnp.int32, (fields, 2 * cap * LANES), 1) // LANES
    wanted = (field == block + cap) | ((field == block) & (block < cap))
    spread = jnp.dot(
        got_ref[:, :fields].astype(jnp.bfloat16),
        jnp.where(wanted, 1.0, 0.0).astype(jnp.bfloat16),
        preferred_element_type=jnp.float32,
    )
    group = 16
    for n in range(sources // group):
        blocks = [
            spread[n * group : (n + 1) * group, c * LANES : (c + 1) * LANES]
            for c in range(2 * cap)
        ]
        rows, scales = blocks[:cap], blocks[cap:]
        same = {(c, d): rows[c] == rows[d] for d in range(cap) for c in range(d)}
        totals = list(scales)
        for (c, d), match in same.items():
            totals[c] = totals[c] + jnp.where(match, scales[d], 0.0)
            totals[d] = totals[d] + jnp.where(match, scales[c], 0.0)
        scales = [total.astype(jnp.bfloat16) for total in totals]
        rows = [row.astype(jnp.int32).astype(jnp.int16) for row in rows]
        lane = lax.broadcasted_iota(jnp.int32, (group, LANES), 1)
        for k in range(slot_dev // LANES):
            at = (lane + k * LANES).astype(jnp.int16)
            weight = jnp.zeros((group, LANES), jnp.bfloat16)
            for c in range(cap):
                weight = jnp.where(at == rows[c], scales[c], weight)
            table[pl.ds(n * group, group), pl.ds(k * LANES, LANES)] = weight
    parts = chunk // LANES
    for n in range(width // 2 // chunk):
        columns = pl.ds(pl.multiple_of(core * (width // 2) + n * chunk, chunk), chunk)
        summed = jnp.dot(table[...], slab_ref[:, columns], preferred_element_type=jnp.float32)
        summed = summed.astype(out_ref.dtype)
        out_ref[:, pl.ds(n * parts, parts), :] = summed.reshape(sources, parts, LANES)


def add_kernel(got_ref, kept_ref, out_ref):
    out_ref[...] = (got_ref[...].astype(jnp.float32) + kept_ref[...]).astype(out_ref.dtype)


def sum_kernel(got_ref, inputs_ref, out_ref):
    sources, tiles, _ = got_ref.shape
    chips = sources // 2
    memory = jnp.concatenate(
        [
            sum(
                jnp.sum(got_ref[pl.ds(core * chips + n, 8)].astype(jnp.float32), axis=0)
                for n in range(0, chips, 8)
            )
            for core in range(2)
        ],
        axis=0,
    )
    memory = memory.reshape(1, 2 * tiles * LANES)
    out_ref[...] = (inputs_ref[...].astype(jnp.float32) + memory).astype(jnp.bfloat16)


def body(inputs, values, slots, weights):
    owners = lax.axis_size(AXES)
    slot_dev, width = values.shape
    cap = 4 * slots.size // owners
    tiles = width // LANES
    chunk = 2048
    vmem = pl.BlockSpec(memory_space=pltpu.VMEM)
    hbm = pl.BlockSpec(memory_space=pltpu.HBM)

    def call(kernel, shapes, specs, name, scratch=()):
        return pl.pallas_call(
            kernel,
            out_shape=[pltpu.VMEM(*shape) for shape in shapes],
            in_specs=specs,
            out_specs=[vmem] * len(shapes),
            scratch_shapes=scratch,
            compiler_params=pltpu.CompilerParams(vmem_limit_bytes=24 * MIB),
            name=name,
        )

    constrain = pltpu.with_memory_space_constraint
    (packed,) = call(
        lambda *refs: request_kernel(owners, cap, *refs),
        [((owners, LANES), jnp.float32)],
        [hbm] * 3,
        "request",
        [
            pltpu.VMEM(slots.shape, slots.dtype),
            pltpu.VMEM(weights.shape, weights.dtype),
            pltpu.SemaphoreType.DMA((2,)),
        ],
    )(*[constrain(array, pltpu.HBM) for array in (slots, weights, values)])
    got = lax.all_to_all(
        packed.reshape(owners, 1, LANES), GROUP, split_axis=0, concat_axis=0, tiled=True
    ).reshape(owners, LANES)
    half = (owners, tiles // 2, LANES)
    slab = constrain(values, pltpu.VMEM)
    other, own = [
        call(
            lambda *refs, other=other: half_kernel(cap, chunk, other, *refs),
            [(half, jnp.bfloat16 if other else jnp.float32)],
            [vmem] * 2,
            "other_half" if other else "own_half",
            [pltpu.VMEM((owners, slot_dev), jnp.bfloat16)],
        )(got, slab)[0]
        for other in (True, False)
    ]
    swapped = lax.ppermute(other, "core", [(0, 1), (1, 0)])
    (partials,) = call(add_kernel, [(half, jnp.bfloat16)], [vmem] * 2, "add")(swapped, own)
    returned = lax.all_to_all(partials, GROUP, split_axis=0, concat_axis=0, tiled=True)
    return pl.pallas_call(
        sum_kernel,
        out_shape=jax.ShapeDtypeStruct(inputs.shape, jnp.bfloat16),
        in_specs=[vmem] * 2,
        out_specs=vmem,
        compiler_params=pltpu.CompilerParams(vmem_limit_bytes=24 * MIB),
        name="sum",
    )(returned, inputs)


def solution(mesh):
    hst, chip = mesh.devices.shape
    mesh = Mesh(mesh.devices.reshape(hst // 2, 2, 4, chip // 4), AXES)
    in_specs = (P(AXES, None), P(AXES, None), P(AXES, None, None), P(AXES, None, None))
    return jax.shard_map(
        body, mesh=mesh, in_specs=in_specs, out_specs=P(AXES, None), check_vma=False
    )
```

```python
import jax
import jax.numpy as jnp
from jax import lax
from jax.experimental import pallas as pl
from jax.experimental.pallas import tpu as pltpu
from jax.sharding import Mesh, PartitionSpec as P

AXES = ("y", "core", "z", "x")
CHIPS = ("x", "z", "y")
GROUP = ("core", *CHIPS)
LANES = 128
MIB = 1024 * 1024


def request_kernel(
    owners, cap, slots_hbm, weights_hbm, values_hbm, out_ref, slots_ref, weights_ref, sems
):
    slot_dev = values_hbm.shape[0]
    copies = [
        pltpu.make_async_copy(slots_hbm, slots_ref, sems.at[0]),
        pltpu.make_async_copy(weights_hbm, weights_ref, sems.at[1]),
    ]
    for copy in copies:
        copy.start()
    for copy in copies:
        copy.wait()
    heads = slots_ref.shape[1]
    slots = slots_ref[0]
    weights = weights_ref[0].astype(jnp.float32)
    slots = jnp.concatenate([slots[h : h + 1] for h in range(heads)], axis=1)
    weights = jnp.concatenate([weights[h : h + 1] for h in range(heads)], axis=1)
    picks = slots.shape[1]
    owner = slots // slot_dev
    row = slots - owner * slot_dev
    low = row % 32
    high = row - low
    xs, zs, ys = (lax.axis_size(axis) for axis in CHIPS)
    y, core = owner // (2 * zs * xs), owner // (zs * xs) % 2
    z, x = owner // xs % zs, owner % xs
    owner = ((core * xs + x) * zs + z) * ys + y
    mine = owner == lax.broadcasted_iota(jnp.int32, (owners, picks), 0)
    before = lax.broadcasted_iota(jnp.int32, (picks, picks), 0) < lax.broadcasted_iota(
        jnp.int32, (picks, picks), 1
    )
    marks = jnp.where(mine, 1.0, 0.0).astype(jnp.bfloat16)
    earlier = jnp.dot(
        marks,
        jnp.where(before, 1.0, 0.0).astype(jnp.bfloat16),
        preferred_element_type=jnp.float32,
    )
    rank = jnp.sum(jnp.where(mine, earlier, 0.0), axis=0, keepdims=True).astype(jnp.int32)
    lane = lax.broadcasted_iota(jnp.int32, (4 * cap, picks), 0) - rank
    fields = jnp.where(
        lane == 0,
        high.astype(jnp.float32),
        jnp.where(
            lane == cap, low.astype(jnp.float32), jnp.where(lane == 2 * cap, weights, 0.0)
        ),
    )
    total = lax.dot_general(
        marks,
        fields.astype(jnp.bfloat16),
        (((1,), (1,)), ((), ())),
        preferred_element_type=jnp.float32,
    )
    rest = jnp.zeros((owners, LANES - 4 * cap), jnp.float32)
    out_ref[...] = jnp.concatenate([total, rest], axis=1)


def half_kernel(cap, chunk, other, got_ref, slab_ref, out_ref, table):
    slot_dev, width = slab_ref.shape
    sources = got_ref.shape[0]
    core = lax.axis_index("core")
    core = 1 - core if other else core
    fields = 4 * cap
    field = lax.broadcasted_iota(jnp.int32, (fields, 2 * cap * LANES), 0)
    block = lax.broadcasted_iota(jnp.int32, (fields, 2 * cap * LANES), 1) // LANES
    wanted = (field == block + cap) | ((field == block) & (block < cap))
    spread = jnp.dot(
        got_ref[:, :fields].astype(jnp.bfloat16),
        jnp.where(wanted, 1.0, 0.0).astype(jnp.bfloat16),
        preferred_element_type=jnp.float32,
    )
    group = 16
    for n in range(sources // group):
        blocks = [
            spread[n * group : (n + 1) * group, c * LANES : (c + 1) * LANES]
            for c in range(2 * cap)
        ]
        rows, scales = blocks[:cap], blocks[cap:]
        same = {(c, d): rows[c] == rows[d] for d in range(cap) for c in range(d)}
        totals = list(scales)
        for (c, d), match in same.items():
            totals[c] = totals[c] + jnp.where(match, scales[d], 0.0)
            totals[d] = totals[d] + jnp.where(match, scales[c], 0.0)
        scales = [total.astype(jnp.bfloat16) for total in totals]
        rows = [row.astype(jnp.int32).astype(jnp.int16) for row in rows]
        lane = lax.broadcasted_iota(jnp.int32, (group, LANES), 1)
        for k in range(slot_dev // LANES):
            at = (lane + k * LANES).astype(jnp.int16)
            weight = jnp.zeros((group, LANES), jnp.bfloat16)
            for c in range(cap):
                weight = jnp.where(at == rows[c], scales[c], weight)
            table[pl.ds(n * group, group), pl.ds(k * LANES, LANES)] = weight
    parts = chunk // LANES
    for n in range(width // 2 // chunk):
        columns = pl.ds(pl.multiple_of(core * (width // 2) + n * chunk, chunk), chunk)
        summed = jnp.dot(table[...], slab_ref[:, columns], preferred_element_type=jnp.float32)
        summed = summed.astype(out_ref.dtype)
        out_ref[:, pl.ds(n * parts, parts), :] = summed.reshape(sources, parts, LANES)


def add_kernel(got_ref, kept_ref, out_ref):
    out_ref[...] = (got_ref[...].astype(jnp.float32) + kept_ref[...]).astype(out_ref.dtype)


def sum_kernel(got_ref, inputs_ref, out_ref):
    sources, tiles, _ = got_ref.shape
    chips = sources // 2
    memory = jnp.concatenate(
        [
            sum(
                jnp.sum(got_ref[pl.ds(core * chips + n, 8)].astype(jnp.float32), axis=0)
                for n in range(0, chips, 8)
            )
            for core in range(2)
        ],
        axis=0,
    )
    memory = memory.reshape(1, 2 * tiles * LANES)
    out_ref[...] = (inputs_ref[...].astype(jnp.float32) + memory).astype(jnp.bfloat16)


def body(inputs, values, slots, weights):
    owners = lax.axis_size(AXES)
    slot_dev, width = values.shape
    cap = 4 * slots.size // owners
    tiles = width // LANES
    chunk = 2048
    vmem = pl.BlockSpec(memory_space=pltpu.VMEM)
    hbm = pl.BlockSpec(memory_space=pltpu.HBM)

    def call(kernel, shapes, specs, name, scratch=()):
        return pl.pallas_call(
            kernel,
            out_shape=[pltpu.VMEM(*shape) for shape in shapes],
            in_specs=specs,
            out_specs=[vmem] * len(shapes),
            scratch_shapes=scratch,
            compiler_params=pltpu.CompilerParams(vmem_limit_bytes=24 * MIB),
            name=name,
        )

    constrain = pltpu.with_memory_space_constraint
    (packed,) = call(
        lambda *refs: request_kernel(owners, cap, *refs),
        [((owners, LANES), jnp.float32)],
        [hbm] * 3,
        "request",
        [
            pltpu.VMEM(slots.shape, slots.dtype),
            pltpu.VMEM(weights.shape, weights.dtype),
            pltpu.SemaphoreType.DMA((2,)),
        ],
    )(*[constrain(array, pltpu.HBM) for array in (slots, weights, values)])
    got = lax.all_to_all(
        packed.reshape(owners, 1, LANES), GROUP, split_axis=0, concat_axis=0, tiled=True
    ).reshape(owners, LANES)
    half = (owners, tiles // 2, LANES)
    slab = constrain(values, pltpu.VMEM)
    other, own = [
        call(
            lambda *refs, other=other: half_kernel(cap, chunk, other, *refs),
            [(half, jnp.bfloat16 if other else jnp.float32)],
            [vmem] * 2,
            "other_half" if other else "own_half",
            [pltpu.VMEM((owners, slot_dev), jnp.bfloat16)],
        )(got, slab)[0]
        for other in (True, False)
    ]
    swapped = lax.ppermute(other, "core", [(0, 1), (1, 0)])
    (partials,) = call(add_kernel, [(half, jnp.bfloat16)], [vmem] * 2, "add")(swapped, own)
    returned = lax.all_to_all(partials, GROUP, split_axis=0, concat_axis=0, tiled=True)
    return pl.pallas_call(
        sum_kernel,
        out_shape=jax.ShapeDtypeStruct(inputs.shape, jnp.bfloat16),
        in_specs=[vmem] * 2,
        out_specs=vmem,
        compiler_params=pltpu.CompilerParams(vmem_limit_bytes=24 * MIB),
        name="sum",
    )(returned, inputs)


def solution(mesh):
    hst, chip = mesh.devices.shape
    mesh = Mesh(mesh.devices.reshape(hst // 2, 2, 4, chip // 4), AXES)
    in_specs = (P(AXES, None), P(AXES, None), P(AXES, None, None), P(AXES, None, None))
    return jax.shard_map(
        body, mesh=mesh, in_specs=in_specs, out_specs=P(AXES, None), check_vma=False
    )
```

```python
import jax
import jax.numpy as jnp
from jax import lax
from jax.experimental import pallas as pl
from jax.experimental.pallas import tpu as pltpu
from jax.sharding import Mesh, PartitionSpec as P

AXES = ("y", "core", "z", "x")
CHIPS = ("x", "z", "y")
GROUP = ("core", *CHIPS)
LANES = 128
MIB = 1024 * 1024


def request_kernel(
    owners, cap, slots_hbm, weights_hbm, values_hbm, out_ref, slots_ref, weights_ref, sems
):
    slot_dev = values_hbm.shape[0]
    copies = [
        pltpu.make_async_copy(slots_hbm, slots_ref, sems.at[0]),
        pltpu.make_async_copy(weights_hbm, weights_ref, sems.at[1]),
    ]
    for copy in copies:
        copy.start()
    for copy in copies:
        copy.wait()
    heads = slots_ref.shape[1]
    slots = slots_ref[0]
    weights = weights_ref[0].astype(jnp.float32)
    slots = jnp.concatenate([slots[h : h + 1] for h in range(heads)], axis=1)
    weights = jnp.concatenate([weights[h : h + 1] for h in range(heads)], axis=1)
    picks = slots.shape[1]
    owner = slots // slot_dev
    row = slots - owner * slot_dev
    low = row % 32
    high = row - low
    xs, zs, ys = (lax.axis_size(axis) for axis in CHIPS)
    y, core = owner // (2 * zs * xs), owner // (zs * xs) % 2
    z, x = owner // xs % zs, owner % xs
    owner = ((core * xs + x) * zs + z) * ys + y
    mine = owner == lax.broadcasted_iota(jnp.int32, (owners, picks), 0)
    before = lax.broadcasted_iota(jnp.int32, (picks, picks), 0) < lax.broadcasted_iota(
        jnp.int32, (picks, picks), 1
    )
    marks = jnp.where(mine, 1.0, 0.0).astype(jnp.bfloat16)
    earlier = jnp.dot(
        marks,
        jnp.where(before, 1.0, 0.0).astype(jnp.bfloat16),
        preferred_element_type=jnp.float32,
    )
    rank = jnp.sum(jnp.where(mine, earlier, 0.0), axis=0, keepdims=True).astype(jnp.int32)
    lane = lax.broadcasted_iota(jnp.int32, (4 * cap, picks), 0) - rank
    fields = jnp.where(
        lane == 0,
        high.astype(jnp.float32),
        jnp.where(
            lane == cap, low.astype(jnp.float32), jnp.where(lane == 2 * cap, weights, 0.0)
        ),
    )
    total = lax.dot_general(
        marks,
        fields.astype(jnp.bfloat16),
        (((1,), (1,)), ((), ())),
        preferred_element_type=jnp.float32,
    )
    rest = jnp.zeros((owners, LANES - 4 * cap), jnp.float32)
    out_ref[...] = jnp.concatenate([total, rest], axis=1)


def half_kernel(cap, chunk, other, got_ref, slab_ref, out_ref, table):
    slot_dev, width = slab_ref.shape
    sources = got_ref.shape[0]
    core = lax.axis_index("core")
    core = 1 - core if other else core
    fields = 4 * cap
    field = lax.broadcasted_iota(jnp.int32, (fields, 2 * cap * LANES), 0)
    block = lax.broadcasted_iota(jnp.int32, (fields, 2 * cap * LANES), 1) // LANES
    wanted = (field == block + cap) | ((field == block) & (block < cap))
    spread = jnp.dot(
        got_ref[:, :fields].astype(jnp.bfloat16),
        jnp.where(wanted, 1.0, 0.0).astype(jnp.bfloat16),
        preferred_element_type=jnp.float32,
    )
    group = 16
    for n in range(sources // group):
        blocks = [
            spread[n * group : (n + 1) * group, c * LANES : (c + 1) * LANES]
            for c in range(2 * cap)
        ]
        rows, scales = blocks[:cap], blocks[cap:]
        same = {(c, d): rows[c] == rows[d] for d in range(cap) for c in range(d)}
        totals = list(scales)
        for (c, d), match in same.items():
            totals[c] = totals[c] + jnp.where(match, scales[d], 0.0)
            totals[d] = totals[d] + jnp.where(match, scales[c], 0.0)
        scales = [total.astype(jnp.bfloat16) for total in totals]
        rows = [row.astype(jnp.int32).astype(jnp.int16) for row in rows]
        lane = lax.broadcasted_iota(jnp.int32, (group, LANES), 1)
        for k in range(slot_dev // LANES):
            at = (lane + k * LANES).astype(jnp.int16)
            weight = jnp.zeros((group, LANES), jnp.bfloat16)
            for c in range(cap):
                weight = jnp.where(at == rows[c], scales[c], weight)
            table[pl.ds(n * group, group), pl.ds(k * LANES, LANES)] = weight
    parts = chunk // LANES
    for n in range(width // 2 // chunk):
        columns = pl.ds(pl.multiple_of(core * (width // 2) + n * chunk, chunk), chunk)
        summed = jnp.dot(table[...], slab_ref[:, columns], preferred_element_type=jnp.float32)
        summed = summed.astype(out_ref.dtype)
        out_ref[:, pl.ds(n * parts, parts), :] = summed.reshape(sources, parts, LANES)


def add_kernel(got_ref, kept_ref, out_ref):
    out_ref[...] = (got_ref[...].astype(jnp.float32) + kept_ref[...]).astype(out_ref.dtype)


def sum_kernel(got_ref, inputs_ref, out_ref):
    sources, tiles, _ = got_ref.shape
    chips = sources // 2
    memory = jnp.concatenate(
        [
            sum(
                jnp.sum(got_ref[pl.ds(core * chips + n, 16)].astype(jnp.float32), axis=0)
                for n in range(0, chips, 16)
            )
            for core in range(2)
        ],
        axis=0,
    )
    memory = memory.reshape(1, 2 * tiles * LANES)
    out_ref[...] = (inputs_ref[...].astype(jnp.float32) + memory).astype(jnp.bfloat16)


def body(inputs, values, slots, weights):
    owners = lax.axis_size(AXES)
    slot_dev, width = values.shape
    cap = 4 * slots.size // owners
    tiles = width // LANES
    chunk = 2048
    vmem = pl.BlockSpec(memory_space=pltpu.VMEM)
    hbm = pl.BlockSpec(memory_space=pltpu.HBM)

    def call(kernel, shapes, specs, name, scratch=()):
        return pl.pallas_call(
            kernel,
            out_shape=[pltpu.VMEM(*shape) for shape in shapes],
            in_specs=specs,
            out_specs=[vmem] * len(shapes),
            scratch_shapes=scratch,
            compiler_params=pltpu.CompilerParams(vmem_limit_bytes=24 * MIB),
            name=name,
        )

    constrain = pltpu.with_memory_space_constraint
    (packed,) = call(
        lambda *refs: request_kernel(owners, cap, *refs),
        [((owners, LANES), jnp.float32)],
        [hbm] * 3,
        "request",
        [
            pltpu.VMEM(slots.shape, slots.dtype),
            pltpu.VMEM(weights.shape, weights.dtype),
            pltpu.SemaphoreType.DMA((2,)),
        ],
    )(*[constrain(array, pltpu.HBM) for array in (slots, weights, values)])
    got = lax.all_to_all(
        packed.reshape(owners, 1, LANES), GROUP, split_axis=0, concat_axis=0, tiled=True
    ).reshape(owners, LANES)
    half = (owners, tiles // 2, LANES)
    slab = constrain(values, pltpu.VMEM)
    other, own = [
        call(
            lambda *refs, other=other: half_kernel(cap, chunk, other, *refs),
            [(half, jnp.bfloat16 if other else jnp.float32)],
            [vmem] * 2,
            "other_half" if other else "own_half",
            [pltpu.VMEM((owners, slot_dev), jnp.bfloat16)],
        )(got, slab)[0]
        for other in (True, False)
    ]
    swapped = lax.ppermute(other, "core", [(0, 1), (1, 0)])
    (partials,) = call(add_kernel, [(half, jnp.bfloat16)], [vmem] * 2, "add")(swapped, own)
    returned = lax.all_to_all(partials, GROUP, split_axis=0, concat_axis=0, tiled=True)
    return pl.pallas_call(
        sum_kernel,
        out_shape=jax.ShapeDtypeStruct(inputs.shape, jnp.bfloat16),
        in_specs=[vmem] * 2,
        out_specs=vmem,
        compiler_params=pltpu.CompilerParams(vmem_limit_bytes=24 * MIB),
        name="sum",
    )(returned, inputs)


def solution(mesh):
    hst, chip = mesh.devices.shape
    mesh = Mesh(mesh.devices.reshape(hst // 2, 2, 4, chip // 4), AXES)
    in_specs = (P(AXES, None), P(AXES, None), P(AXES, None, None), P(AXES, None, None))
    return jax.shard_map(
        body, mesh=mesh, in_specs=in_specs, out_specs=P(AXES, None), check_vma=False
    )
```
